32 devices in a mesh: row: 2 (over y), vocab: 16 (over z, x, core).
Axes of the slice: x: 2, y: 2, z: 4, core: 2. Of those that a mesh axis runs over, the one named last changes fastest.
Arguments:
- tokens: bfloat16 [320, 7168], P(('row', 'vocab')), may hold values from -60 to 60
- norm_gain: float32 [7168], replicated, may hold values from 0.5 to 1.5
- router: bfloat16 [7168, 16], replicated, may hold values from -0.0625 to 0.0625
- routes: int32 [320, 8], P(('row', 'vocab')), may hold values from 0 to 15, all different within a row; in each aligned block of 10 rows (0 to 9, 10 to 19, ...) at most 5 rows name the same one
- w_gate: bfloat16 [16, 7168, 1024], P('vocab', None, 'row'), may hold values from -0.0625 to 0.0625
- w_up: bfloat16 [16, 7168, 1024], P('vocab', None, 'row'), may hold values from -0.0625 to 0.0625
- w_down: bfloat16 [16, 1024, 7168], P('vocab', 'row'), may hold values from -0.1875 to 0.1875
- head_gain: float32 [7168], replicated, may hold values from 0.5 to 1.5
- head: bfloat16 [65536, 7168], P(('row', 'vocab')), may hold values from -0.18 to 0.18
- draft_logits: bfloat16 [64, 4, 65536], P(None, None, ('row', 'vocab')), may hold values from -18 to 235
- draft_tokens: int32 [64, 4], replicated, may hold values from 0 to 65535
- reject_pos: int32 [64], replicated, may hold values from 0 to 4
Outputs:
- residual: float32 [64, 65536], P(None, ('row', 'vocab'))
- accept: float32 [64, 4], replicated
The draws below stay inside these ranges and needn't reach their ends.
Inputs may be any that keep to these rules, and one draw needn't show every extreme that they name: `routes`: each row names 8 different experts. Among the rows of one device no expert is named more than 5 times, and some device's rows name some expert exactly 5 times.
All inputs are finite; a program needn't handle non-finite values.
Results may differ from the reference program's by a relative error of at most 0.012.
Values may be sent and summed in bfloat16 or wider, within the bound.
A program may use at most 256 MiB of HBM per device.

```python
import math
import jax
import jax.numpy as jnp
import numpy as np
from jax import lax

D = 7168
FF = 1024
V = 65536
TOP = 8
DRAFTS = 4
SLOTS = 5
ROWS_DEV = 10
REQ = 64
ROWS = 320
EXPERTS = 16
CAP = 5
N_ROW = 2
N_VOCAB = 16


def reject_helper(key):
    return jax.random.randint(jax.random.fold_in(key, 31), (REQ,), 0, DRAFTS + 1)


def draw_reject_pos(key, part):
    return reject_helper(key).astype(jnp.int32)


def draw_tokens(key, part):
    base_vals = jax.random.normal(jax.random.fold_in(key, 1), (ROWS, D))
    row_scale = jnp.exp(jax.random.uniform(jax.random.fold_in(key, 2), (ROWS, 1), minval=math.log(0.5), maxval=math.log(5.0)))
    col_scale = jnp.exp(jax.random.uniform(jax.random.fold_in(key, 3), (1, D), minval=math.log(0.4), maxval=math.log(2.5)))
    values = jnp.clip(base_vals * row_scale * col_scale, -60.0, 60.0)
    return values.astype(jnp.bfloat16)


def draw_head(key, part):
    spread = 3.0 / math.sqrt(D)
    base_vals = jax.random.normal(jax.random.fold_in(key, 11), (V, D)) * spread
    return jnp.clip(base_vals, -0.18, 0.18).astype(jnp.bfloat16)


def draw_draft_logits(key, part):
    base_vals = jnp.clip(3.0 * jax.random.normal(jax.random.fold_in(key, 21), (REQ, DRAFTS, V)), -18.0, 18.0)
    return base_vals.astype(jnp.bfloat16)


def plant(result, own_key, smallest, high):
    shape = result.shape
    place = [jax.random.randint(jax.random.fold_in(own_key, axis), (), 0, shape[axis]) for axis in range(len(shape))]
    result = result.at[tuple(place)].set(smallest)
    longest = shape.index(max(shape))
    place[longest] = (place[longest] + 1) % shape[longest]
    return result.at[tuple(place)].set(high)


def levels(own_key, shape, cuts, least, top_value):
    level = 1.0
    for dim, shards_of in cuts:
        draws = jax.random.uniform(jax.random.fold_in(jax.random.fold_in(own_key, 6), dim), (shards_of,), jnp.float32, least / len(cuts), top_value / len(cuts))
        level = level * jnp.repeat(jnp.exp(draws), shape[dim] // shards_of).reshape((-1,) + (1,) * (len(shape) - 1 - dim))
    return level


def shared_out(stream_key, own, number, rows, number_of, top, most, slope):
    order = jax.random.permutation(stream_key, number_of)
    heavy_load, usual = load_shares(number_of, rows * top, most, slope, True), load_shares(number_of, rows * top, most, slope, False)
    places = jnp.arange(number_of)

    def named(tallies, offset_by):
        used = int((tallies > 0).sum())
        fixed = max(1, used // 4)
        shifted = fixed + (places - fixed + offset_by * (used - fixed)) % max(1, number_of - fixed)
        return jnp.zeros((number_of,), jnp.int32).at[order[jnp.where(places < fixed, places, shifted)]].set(jnp.asarray(tallies, jnp.int32))

    tallies = jnp.where(number % 4 == 0, named(heavy_load, number // 4), named(usual, number - number // 4 - 1))
    mixed = jax.random.permutation(jax.random.fold_in(own, 3), number_of)
    donor, sink = mixed[0:number_of // 2 * 2:2], mixed[1:number_of // 2 * 2:2]
    slack = jnp.minimum(tallies[donor] - 1, most - tallies[sink]) // 2
    slack = jnp.where((donor == order[0]) | (sink == order[0]) | (tallies[sink] == 0), 0, jnp.maximum(slack, 0))
    shifted = jax.random.randint(jax.random.fold_in(own, 4), (number_of // 2,), 0, 1 << 20) % (slack + 1)
    tallies = tallies.at[donor].add(-shifted).at[sink].add(shifted)
    members = jnp.searchsorted(jnp.cumsum(tallies), jnp.arange(rows * top), side="right").astype(jnp.int32)
    table = members.reshape(top, rows).T
    table = table[jax.random.permutation(jax.random.fold_in(own, 1), rows)]
    offset_by = jax.random.randint(jax.random.fold_in(own, 2), (rows, 1), 0, top)
    return jnp.take_along_axis(table, (jnp.arange(top)[None, :] + offset_by) % top, axis=1)


def load_shares(amount, total, most, slope, full):
    portions = [(1 << 20) // math.isqrt(grade ** slope) + 1 for grade in range(1, amount + 1)]
    largest = most if full else min(most, max(-(-total // amount), total * portions[0] // sum(portions)))
    least = 1 if total - largest >= amount - 1 else 0
    given, spare = [largest] + [least] * (amount - 1), total - largest - least * (amount - 1)
    while spare > 0:
        candidates = [i for i in range(1, amount) if given[i] < largest] or [i for i in range(1, amount) if given[i] < most]
        pool, budget = sum([portions[i] for i in candidates]), spare
        for i in candidates:
            more = min(most - given[i], max(1, budget * portions[i] // pool), spare)
            given[i] = given[i] + more
            spare = spare - more
    return np.array(given)


def centred(key, shape, deviation, most, split=(), kind=jnp.bfloat16):
    level = levels(key, shape, split, -0.22, 0.18) if split else 1.0
    drawn = jax.random.normal(key, shape, jnp.float32) * deviation * level
    return jnp.minimum(jnp.maximum(drawn, -most), most).astype(kind)


def setup_inputs(seed: int = 0) -> dict:
    splits = jax.random.split(jax.random.key(seed), 13)
    tokens = draw_tokens(jax.random.fold_in(splits[12], 71), 0)
    norm_gain = jnp.clip(1.0 + 0.1 * jax.random.normal(splits[1], (D,), jnp.float32), 0.5, 1.5)
    router = centred(splits[2], (D, EXPERTS), D ** -0.5, 0.0625)
    routes_keys = jax.random.split(jax.random.fold_in(splits[3], 1), ROWS // ROWS_DEV)
    routes_turns = jax.random.permutation(jax.random.fold_in(splits[3], 3), ROWS // ROWS_DEV)
    routes = jax.vmap(lambda own, number: shared_out(jax.random.fold_in(splits[3], 2), own, number, ROWS_DEV, EXPERTS, TOP, CAP, 1))(routes_keys, routes_turns).reshape((ROWS, TOP))
    w_gate = centred(splits[4], (EXPERTS, D, FF), D ** -0.5, 0.0625, ((0, 16), (2, 2)))
    w_up = centred(splits[5], (EXPERTS, D, FF), D ** -0.5, 0.0625, ((0, 16), (2, 2)))
    w_down = centred(splits[6], (EXPERTS, FF, D), FF ** -0.5, 0.1875, ((0, 16), (1, 2)))
    head_gain = jnp.clip(1.0 + 0.1 * jax.random.normal(splits[7], (D,), jnp.float32), 0.5, 1.5)
    head = draw_head(jax.random.fold_in(splits[12], 71), 0)
    draft_logits = draw_draft_logits(jax.random.fold_in(splits[12], 71), 0)
    draft_tokens = plant(jax.random.randint(splits[10], (REQ, DRAFTS), 0, V), jax.random.fold_in(splits[10], 1), 0, V - 1).astype(jnp.int32)
    reject_pos = draw_reject_pos(jax.random.fold_in(splits[12], 71), 0)
    return dict(tokens=tokens, norm_gain=norm_gain, router=router, routes=routes, w_gate=w_gate, w_up=w_up, w_down=w_down, head_gain=head_gain, head=head, draft_logits=draft_logits, draft_tokens=draft_tokens, reject_pos=reject_pos)


def rms_norm(values, gain):
    return values * lax.rsqrt(lax.optimization_barrier(jnp.mean(values * values, axis=-1, keepdims=True)) + 1e-06) * gain

def reference(tokens, norm_gain, router, routes, w_gate, w_up, w_down, head_gain, head, draft_logits, draft_tokens, reject_pos):
    resid_in = tokens.astype(jnp.float32)
    normed = rms_norm(resid_in, norm_gain).astype(jnp.bfloat16)
    scores = jax.nn.sigmoid(jnp.dot(normed, router, preferred_element_type=jnp.float32))
    picked = jnp.take_along_axis(scores, routes, axis=1)
    weights = 2.5 * picked / lax.optimization_barrier(jnp.sum(picked, axis=1, keepdims=True))
    ff_part = FF // N_ROW
    most_rows = min(ROWS, CAP * N_ROW * N_VOCAB)

    def one_expert(moe_sum, expert):
        hit_mask = routes == expert
        named_rows = jnp.any(hit_mask, axis=1)
        row_idx = jnp.nonzero(named_rows, size=most_rows, fill_value=0)[0].astype(jnp.int32)
        valid_rows = (jnp.arange(most_rows) < jnp.sum(named_rows.astype(jnp.int32))).astype(jnp.float32)
        chosen = normed[row_idx]
        gate_out = jnp.dot(chosen, w_gate[expert], preferred_element_type=jnp.float32)
        up_out = jnp.dot(chosen, w_up[expert], preferred_element_type=jnp.float32)
        hidden = (jax.nn.silu(gate_out) * up_out).astype(jnp.bfloat16)
        down_all = w_down[expert]
        part_sum = jnp.zeros((most_rows, D), jnp.float32)
        for block in range(N_ROW):
            part_term = jnp.dot(hidden[:, block * ff_part:(block + 1) * ff_part], down_all[block * ff_part:(block + 1) * ff_part], preferred_element_type=jnp.float32).astype(jnp.bfloat16)
            part_term = lax.optimization_barrier(part_term)
            part_sum = part_sum + part_term.astype(jnp.float32)
        expert_out = lax.optimization_barrier(part_sum.astype(jnp.bfloat16)).astype(jnp.float32)
        row_weight = lax.optimization_barrier(jnp.sum(jnp.where(hit_mask, weights, 0.0), axis=1))[row_idx] * valid_rows
        return (moe_sum.at[row_idx].add(row_weight[:, None] * expert_out), None)
    moe_sum, _ = lax.scan(one_expert, jnp.zeros((ROWS, D), jnp.float32), jnp.arange(EXPERTS, dtype=jnp.int32))
    mixed_rows = resid_in + moe_sum
    final_normed = rms_norm(mixed_rows, head_gain).astype(jnp.bfloat16)
    logits = lax.dot_general(final_normed, head, (((1,), (1,)), ((), ())), preferred_element_type=jnp.float32)
    logits = logits.reshape(REQ, SLOTS, V)
    top_target = lax.optimization_barrier(jnp.max(logits, axis=-1, keepdims=True))
    sum_target = lax.optimization_barrier(jnp.sum(jnp.exp(logits - top_target), axis=-1, keepdims=True))
    target = jnp.exp(logits - top_target) / sum_target
    draft_vals = draft_logits.astype(jnp.float32)
    top_draft = lax.optimization_barrier(jnp.max(draft_vals, axis=-1, keepdims=True))
    sum_draft = lax.optimization_barrier(jnp.sum(jnp.exp(draft_vals - top_draft), axis=-1, keepdims=True))
    draft_prob = jnp.exp(draft_vals - top_draft) / sum_draft
    pick_target = jnp.take_along_axis(logits[:, :DRAFTS], draft_tokens[:, :, None], axis=2)[:, :, 0]
    pick_draft = jnp.take_along_axis(draft_vals, draft_tokens[:, :, None], axis=2)[:, :, 0]
    log_target = pick_target - top_target[:, :DRAFTS, 0] - jnp.log(sum_target[:, :DRAFTS, 0])
    log_draft = pick_draft - top_draft[:, :, 0] - jnp.log(sum_draft[:, :, 0])
    accept = jnp.exp(jnp.minimum(log_target - log_draft, 0.0))
    position = (jnp.arange(SLOTS, dtype=jnp.int32)[None, :] == reject_pos[:, None]).astype(jnp.float32)
    target_at = lax.optimization_barrier(jnp.sum(position[:, :, None] * target, axis=1))
    draft_pad = jnp.concatenate([draft_prob, jnp.zeros((REQ, 1, V), jnp.float32)], axis=1)
    draft_at = lax.optimization_barrier(jnp.sum(position[:, :, None] * draft_pad, axis=1))
    gap_rows = jnp.maximum(target_at - draft_at, 0.0)
    residual = jnp.sqrt(V * gap_rows / lax.optimization_barrier(jnp.sum(gap_rows, axis=-1, keepdims=True)))
    return (residual, accept)
```

```python
import functools

import jax
import jax.numpy as jnp
from jax import lax
from jax.experimental import pallas as pl
from jax.experimental.pallas import tpu as pltpu
from jax.sharding import PartitionSpec as P

V = 65536
DRAFTS = 4
MESH = pl.DeviceIdType.MESH
VMEM = pltpu.VMEM
Z = 4
CHIPS = 16
CUT = 2304


def rms_norm(values, gain):
    return values * lax.rsqrt(jnp.mean(values * values, axis=-1, keepdims=True) + 1e-06) * gain


def place():
    y = lax.axis_index("row")
    v = lax.axis_index("vocab")
    return y, v // 4, (v // 2) % 2, v % 2


def device(y, z, x, c):
    return (y, (z * 2 + x) * 2 + c)


def offset_of(k):
    return ((k + 1) // 2) * (1 - 2 * ((k + 1) % 2))


def greet():
    y, z, x, c = place()
    barrier = pltpu.get_barrier_semaphore()

    def signal(target):
        pl.semaphore_signal(barrier, inc=1, device_id=target, device_id_type=MESH)

    signal(device(y, z, x, 1 - c))
    signal(device(1 - y, z, x, c))
    signal(device(y, z, 1 - x, c))
    pl.when(z + 1 < Z)(lambda: signal(device(y, z + 1, x, c)))
    pl.when(z >= 1)(lambda: signal(device(y, z - 1, x, c)))
    pl.semaphore_wait(barrier, 3 + (z + Z - 1) // Z + (2 * Z - 2 - z) // Z)


def gather_kernel(width, x_ref, o_ref, send_sem, recv_sem):
    y, z, x, c = place()
    halves = (pl.ds(0, CUT), pl.ds(CUT, width - CUT))
    o_ref[y * 8 + z * 2 + x, c] = x_ref[...]
    greet()

    def copy(q, core, h, way, target, stream):
        tile = o_ref.at[q, core, :, halves[h]]
        return pltpu.make_async_remote_copy(
            src_ref=tile,
            dst_ref=tile,
            send_sem=send_sem.at[q, h, way],
            recv_sem=recv_sem.at[q, h, stream],
            device_id=target,
            device_id_type=MESH,
        )

    other = device(y, z, x, 1 - c)

    def visit(k, drain):
        dz = offset_of(k)
        zs = z + dz

        def run(q, h, way, target):
            made = copy(q, c, h, way, target, 1 if way == 0 else 0)
            if drain:
                made.wait_send()
            else:
                made.start()

        @pl.when((zs >= 0) & (zs < Z))
        def _():
            for fx, fy in ((0, 0), (0, 1), (1, 0), (1, 1)):
                q = (1 - y if fy else y) * 8 + zs * 2 + (1 - x if fx else x)
                for h in (0, 1):
                    if not drain:
                        landed = copy(q, c, h, 0, other, 0)
                        if fx or fy:
                            landed.wait_recv()
                        else:
                            pl.when(dz != 0)(landed.wait_recv)
                    if not fx and not fy:
                        pl.when((dz >= 0) & (z >= 1))(lambda: run(q, h, 4, device(y, z - 1, x, c)))
                        pl.when((dz <= 0) & (z + 1 < Z))(lambda: run(q, h, 3, device(y, z + 1, x, c)))
                    if not fy and (h == 0 or not fx):
                        run(q, h, 1, device(1 - y, z, x, c))
                    if not fx and (h == 1 or not fy):
                        run(q, h, 2, device(y, z, 1 - x, c))
                    run(q, h, 0, other)
                    if drain:
                        copy(q, 1 - c, h, 0, other, 1).wait_recv()

    @pl.loop(0, 2 * Z - 1)
    def _(k):
        visit(k, False)

    @pl.loop(0, 2 * Z - 1)
    def _(k):
        visit(k, True)


def gather(block, cid):
    count = lax.axis_size("row") * lax.axis_size("vocab")
    if (lax.axis_size("row"), lax.axis_size("vocab")) != (2, 16):
        return lax.all_gather(block, ("row", "vocab"), axis=0, tiled=False)
    width = block.shape[1]
    out = pl.pallas_call(
        functools.partial(gather_kernel, width),
        out_shape=jax.ShapeDtypeStruct((CHIPS, 2, 16, width), block.dtype),
        in_specs=[pl.BlockSpec(memory_space=VMEM)],
        out_specs=pl.BlockSpec(memory_space=VMEM),
        scratch_shapes=[
            pltpu.SemaphoreType.DMA((CHIPS, 2, 5)),
            pltpu.SemaphoreType.DMA((CHIPS, 2, 2)),
        ],
        compiler_params=pltpu.CompilerParams(
            collective_id=cid, has_side_effects=True, vmem_limit_bytes=40 * 2**20
        ),
    )(block)
    return out.reshape(count, 16, width)


def scatter_kernel(width, p_ref, o_ref, buf, stage, acc, send_sem, recv_sem):
    y, z, x, c = place()
    halves = (pl.ds(0, CUT), pl.ds(CUT, width - CUT))
    sizes = (CUT, width - CUT)
    other = device(y, z, x, 1 - c)
    greet()

    def chip(zs, fx, fy):
        return (1 - y if fy else y) * 8 + zs * 2 + (1 - x if fx else x)

    def to_core(q, h):
        return pltpu.make_async_remote_copy(
            src_ref=p_ref.at[q, 1 - c, :, halves[h]],
            dst_ref=buf.at[0, q, :, halves[h]],
            send_sem=send_sem.at[q, h, 0],
            recv_sem=recv_sem.at[q, h, 0],
            device_id=other,
            device_id_type=MESH,
        )

    def to_parent(q, h, way, target):
        return pltpu.make_async_remote_copy(
            src_ref=stage.at[q, :, halves[h]],
            dst_ref=buf.at[way, q, :, halves[h]],
            send_sem=send_sem.at[q, h, 1],
            recv_sem=recv_sem.at[q, h, way],
            device_id=target,
            device_id_type=MESH,
        )

    flips = ((1, 1), (1, 0), (0, 1), (0, 0))

    def visit(i, phase):
        dz = offset_of(2 * Z - 2 - i)
        zs = z + dz

        @pl.when((zs >= 0) & (zs < Z))
        def _():
            for fx, fy in flips:
                q = chip(zs, fx, fy)
                for h in (0, 1):
                    if phase == 0:
                        to_core(q, h).start()
                        continue
                    if phase == 1:
                        cols = pl.ds(0, sizes[h])

                        def add(way):
                            to_parent(q, h, way, other).wait_recv()
                            acc[:, cols] += buf[way, q, :, halves[h]].astype(jnp.float32)

                        to_core(q, h).wait_recv()
                        acc[:, cols] = p_ref[q, c, :, halves[h]].astype(jnp.float32) + buf[
                            0, q, :, halves[h]
                        ].astype(jnp.float32)
                        if not fy and (h == 0 or not fx):
                            add(1)
                        if not fx and (h == 1 or not fy):
                            add(2)
                        if not fx and not fy:
                            pl.when((dz >= 0) & (z >= 1))(lambda: add(4))
                            pl.when((dz <= 0) & (z + 1 < Z))(lambda: add(3))

                            @pl.when(dz == 0)
                            def _():
                                o_ref[:, halves[h]] = acc[:, cols]

                        stage[q, :, halves[h]] = acc[:, cols].astype(jnp.bfloat16)
                    else:
                        to_core(q, h).wait_send()

                    def run(way, target):
                        made = to_parent(q, h, way, target)
                        if phase == 1:
                            made.start()
                        else:
                            made.wait_send()

                    if fy and (h == 0 or not fx):
                        run(1, device(1 - y, z, x, c))
                    elif fx:
                        run(2, device(y, z, 1 - x, c))
                    else:
                        pl.when(dz > 0)(lambda: run(4, device(y, z + 1, x, c)))
                        pl.when(dz < 0)(lambda: run(3, device(y, z - 1, x, c)))

    for phase in (0, 1, 2):
        pl.loop(0, 2 * Z - 1)(functools.partial(lambda p, i: visit(i, p), phase))


def scatter(parts, cid):
    if (lax.axis_size("row"), lax.axis_size("vocab")) != (2, 16):
        return lax.psum_scatter(
            parts.astype(jnp.float32), ("row", "vocab"), scatter_dimension=0, tiled=False
        )
    width = parts.shape[2]
    return pl.pallas_call(
        functools.partial(scatter_kernel, width),
        out_shape=jax.ShapeDtypeStruct((16, width), jnp.float32),
        in_specs=[pl.BlockSpec(memory_space=VMEM)],
        out_specs=pl.BlockSpec(memory_space=VMEM),
        scratch_shapes=[
            VMEM((5, CHIPS, 16, width), jnp.bfloat16),
            VMEM((CHIPS, 16, width), jnp.bfloat16),
            VMEM((16, CUT), jnp.float32),
            pltpu.SemaphoreType.DMA((CHIPS, 2, 2)),
            pltpu.SemaphoreType.DMA((CHIPS, 2, 5)),
        ],
        compiler_params=pltpu.CompilerParams(
            collective_id=cid, has_side_effects=True, vmem_limit_bytes=40 * 2**20
        ),
    )(parts.reshape(CHIPS, 2, 16, width))


def exchange_kernel(n_vocab, count, x_ref, o_ref, send_sem, recv_sem):
    me = lax.axis_index("row") * n_vocab + lax.axis_index("vocab")
    barrier = pltpu.get_barrier_semaphore()

    @pl.loop(1, count)
    def _(k):
        peer = (me + k) % count
        pl.semaphore_signal(
            barrier, inc=1, device_id=(peer // n_vocab, peer % n_vocab), device_id_type=MESH
        )

    o_ref[me] = x_ref[...]
    pl.semaphore_wait(barrier, count - 1)

    def copy(k, slot):
        peer = (me + k) % count
        return pltpu.make_async_remote_copy(
            src_ref=x_ref,
            dst_ref=o_ref.at[slot],
            send_sem=send_sem.at[k],
            recv_sem=recv_sem.at[k],
            device_id=(peer // n_vocab, peer % n_vocab),
            device_id_type=MESH,
        )

    @pl.loop(1, count)
    def _(k):
        copy(k, me).start()

    @pl.loop(1, count)
    def _(k):
        copy(k, (me + count - k) % count).wait_recv()
        copy(k, me).wait_send()


def exchange(values, cid):
    size = values.shape[0]
    if (lax.axis_size("row"), lax.axis_size("vocab")) != (2, 16):
        return lax.all_gather(values, ("row", "vocab"), axis=0, tiled=False)
    n_vocab = lax.axis_size("vocab")
    count = lax.axis_size("row") * n_vocab
    rows = -(-size // 1024) * 8
    block = jnp.pad(values, (0, rows * 128 - size)).reshape(rows, 128)
    out = pl.pallas_call(
        functools.partial(exchange_kernel, n_vocab, count),
        out_shape=jax.ShapeDtypeStruct((count, rows, 128), jnp.float32),
        in_specs=[pl.BlockSpec(memory_space=VMEM)],
        out_specs=pl.BlockSpec(memory_space=VMEM),
        scratch_shapes=[
            pltpu.SemaphoreType.DMA((count,)),
            pltpu.SemaphoreType.DMA((count,)),
        ],
        compiler_params=pltpu.CompilerParams(collective_id=cid, has_side_effects=True),
    )(block)
    return out.reshape(count, rows * 128)[:, :size]


def pack(rows):
    lead, width = rows.shape[:-2], rows.shape[-1]
    first = rows[..., :8, :]
    main = jnp.concatenate([first[..., : width // 2], first[..., width // 2 :]], axis=-2)
    rest = rows[..., 8:, :].reshape(lead + (16, width // 8))
    return jnp.concatenate([main, rest], axis=-1)


def spread(blocks, width):
    count = blocks.shape[0]
    half = width // 2
    main = jnp.concatenate(
        [blocks[:, :8, :half].reshape(-1, half), blocks[:, 8:, :half].reshape(-1, half)], axis=1
    )
    rest = blocks[:, :, half : half + width // 8].reshape(count * 2, width)
    return jnp.concatenate([main, rest], axis=0)


def unspread(rows, count):
    width = rows.shape[1]
    half = width // 2
    first = rows[: count * 8].reshape(count, 8, width)
    main = jnp.concatenate([first[:, :, :half], first[:, :, half:]], axis=1)
    rest = rows[count * 8 :].reshape(count, 16, width // 8)
    return jnp.concatenate([main, rest], axis=2)


def in_order(per_row, count):
    table = per_row.reshape(count, 10)
    return jnp.concatenate([table[:, :8].reshape(-1), table[:, 8:].reshape(-1)])


def body(
    tokens,
    norm_gain,
    router,
    routes,
    w_gate,
    w_up,
    w_down,
    head_gain,
    head,
    draft_logits,
    draft_tokens,
    reject_pos,
):
    n_vocab = lax.axis_size("vocab")
    count = lax.axis_size("row") * n_vocab
    width = tokens.shape[1]
    packed = width * 5 // 8
    experts = n_vocab
    resid_in = tokens.astype(jnp.float32)
    normed = rms_norm(resid_in, norm_gain).astype(jnp.bfloat16)
    scores = jax.nn.sigmoid(jnp.dot(normed, router, preferred_element_type=jnp.float32))
    member = routes[:, :, None] == jnp.arange(experts, dtype=jnp.int32)[None, None, :]
    picked = jnp.any(member, axis=1).astype(jnp.float32) * scores
    weights = 2.5 * picked / jnp.sum(picked, axis=1, keepdims=True)
    high = lax.reduce_precision(weights, 8, 7)
    low = weights - high
    both = jnp.concatenate([high, low], axis=1).astype(jnp.bfloat16)
    both = jnp.pad(both, ((0, 6), (0, 128 - 2 * experts)))
    gathered = gather(jnp.concatenate([pack(normed), both], axis=1), 0)

    x = spread(gathered, width)
    table = gathered[:, :10, packed : packed + 2 * experts].astype(jnp.float32)
    table = table[:, :, :experts] + table[:, :, experts:]
    mine = jnp.arange(experts, dtype=jnp.int32) == lax.axis_index("vocab")
    row_weight = jnp.sum(jnp.where(mine[None, None, :], table, 0.0), axis=-1)
    row_weight = in_order(row_weight.reshape(-1), count)

    gate_out = jnp.dot(x, w_gate[0], preferred_element_type=jnp.float32)
    up_out = jnp.dot(x, w_up[0], preferred_element_type=jnp.float32)
    hidden = (jax.nn.silu(gate_out) * up_out).astype(jnp.bfloat16)
    down_out = jnp.dot(hidden, w_down[0], preferred_element_type=jnp.float32)
    parts = (down_out * row_weight[:, None]).astype(jnp.bfloat16)
    summed = scatter(unspread(parts, count), 1)

    half = width // 2
    moe_sum = jnp.concatenate(
        [
            jnp.concatenate([summed[:8, :half], summed[8:, :half]], axis=1),
            summed[:, half:].reshape(2, width),
        ],
        axis=0,
    )
    mixed_rows = resid_in + moe_sum
    final_normed = rms_norm(mixed_rows, head_gain).astype(jnp.bfloat16)
    hn = spread(gather(pack(final_normed), 2), width)
    logits = lax.dot_general(
        hn, head, (((1,), (1,)), ((), ())), preferred_element_type=jnp.float32
    )

    local_vocab = head.shape[0]
    requests = draft_tokens.shape[0]
    slots = DRAFTS + 1
    rows = requests * slots
    drafts = requests * DRAFTS
    draft_vals = draft_logits.astype(jnp.float32)
    offset = lax.axis_index(("row", "vocab")) * local_vocab
    lanes = jnp.arange(local_vocab, dtype=jnp.int32)
    local_ids = draft_tokens - offset
    row_ids = in_order(jnp.pad(local_ids, ((0, 0), (0, 1)), constant_values=-1).reshape(-1), count)
    pick_t = jnp.sum(jnp.where(lanes[None, :] == row_ids[:, None], logits, 0.0), axis=-1)
    pick_d = jnp.sum(
        jnp.where(lanes[None, None, :] == local_ids[:, :, None], draft_vals, 0.0), axis=-1
    )
    top_t = jnp.max(logits, axis=-1)
    top_d = jnp.max(draft_vals, axis=-1)
    sum_t = jnp.sum(jnp.exp(logits - top_t[:, None]), axis=-1)
    sum_d = jnp.sum(jnp.exp(draft_vals - top_d[:, :, None]), axis=-1)
    own = [top_t, sum_t, pick_t, top_d.reshape(-1), sum_d.reshape(-1), pick_d.reshape(-1)]
    every = exchange(jnp.concatenate(own), 3)

    def merge(start, size):
        tops = every[:, start : start + size]
        sums = every[:, start + size : start + 2 * size]
        picks = every[:, start + 2 * size : start + 3 * size]
        top = jnp.max(tops, axis=0)
        return top, jnp.sum(sums * jnp.exp(tops - top[None, :]), axis=0), jnp.sum(picks, axis=0)

    top_target, sum_target, pick_target = merge(0, rows)
    top_draft, sum_draft, pick_draft = [
        part.reshape(requests, DRAFTS) for part in merge(3 * rows, drafts)
    ]
    log_draft = pick_draft - top_draft - jnp.log(sum_draft)

    row_at = jnp.arange(requests, dtype=jnp.int32) * slots + reject_pos
    natural = jnp.arange(rows, dtype=jnp.int32)
    order = in_order(natural, count)
    chosen = (row_at[:, None] == order[None, :]).astype(jnp.float32)
    logits_at = jnp.dot(chosen, logits, precision=lax.Precision.HIGHEST)
    top_at = jnp.sum(chosen * top_target[None, :], axis=1)
    sum_at = jnp.sum(chosen * sum_target[None, :], axis=1)
    log_rows = pick_target - top_target - jnp.log(sum_target)
    log_rows = jnp.concatenate(
        [log_rows[: count * 8].reshape(count, 8), log_rows[count * 8 :].reshape(count, 2)], axis=1
    ).reshape(requests, slots)
    accept = jnp.exp(jnp.minimum(log_rows[:, :DRAFTS] - log_draft, 0.0))

    position = jnp.arange(DRAFTS, dtype=jnp.int32)[None, :] == reject_pos[:, None]
    draft_raw = jnp.sum(jnp.where(position[:, :, None], draft_vals, 0.0), axis=1)
    top_d_at = jnp.sum(jnp.where(position, top_draft, 0.0), axis=1)
    sum_d_at = jnp.sum(jnp.where(position, sum_draft, 0.0), axis=1)
    drafted = (reject_pos < DRAFTS)[:, None]
    draft_at = jnp.where(
        drafted, jnp.exp(draft_raw - top_d_at[:, None]) / jnp.where(drafted, sum_d_at[:, None], 1.0), 0.0
    )
    target_at = jnp.exp(logits_at - top_at[:, None]) / sum_at[:, None]
    gap_rows = jnp.maximum(target_at - draft_at, 0.0)
    gap_total = jnp.sum(exchange(jnp.sum(gap_rows, axis=-1), 4), axis=0)
    residual = jnp.sqrt(V * gap_rows / gap_total[:, None])
    return (residual, accept)


def solution(mesh):
    placed = (
        P(("row", "vocab"), None),
        P(),
        P(),
        P(("row", "vocab"), None),
        P("vocab", None, "row"),
        P("vocab", None, "row"),
        P("vocab", "row", None),
        P(),
        P(("row", "vocab"), None),
        P(None, None, ("row", "vocab")),
        P(),
        P(),
    )
    return jax.shard_map(
        body,
        mesh=mesh,
        in_specs=placed,
        out_specs=(P(None, ("row", "vocab")), P()),
        check_vma=False,
    )
```

```python
import functools

import jax
import jax.numpy as jnp
from jax import lax
from jax.experimental import pallas as pl
from jax.experimental.pallas import tpu as pltpu
from jax.sharding import PartitionSpec as P

V = 65536
DRAFTS = 4
MESH = pl.DeviceIdType.MESH
VMEM = pltpu.VMEM
Z = 4
CHIPS = 16
LEVELS = (((0, 0),), ((0, 1), (1, 0)), ((1, 1),))
CUT = 2304


def rms_norm(values, gain):
    return values * lax.rsqrt(jnp.mean(values * values, axis=-1, keepdims=True) + 1e-06) * gain


def place():
    y = lax.axis_index("row")
    v = lax.axis_index("vocab")
    return y, v // 4, (v // 2) % 2, v % 2


def device(y, z, x, c):
    return (y, (z * 2 + x) * 2 + c)


def offset_of(k):
    return ((k + 1) // 2) * (1 - 2 * ((k + 1) % 2))


def greet():
    y, z, x, c = place()
    barrier = pltpu.get_barrier_semaphore()

    def signal(target):
        pl.semaphore_signal(barrier, inc=1, device_id=target, device_id_type=MESH)

    signal(device(y, z, x, 1 - c))
    signal(device(1 - y, z, x, c))
    signal(device(y, z, 1 - x, c))
    pl.when(z + 1 < Z)(lambda: signal(device(y, z + 1, x, c)))
    pl.when(z >= 1)(lambda: signal(device(y, z - 1, x, c)))
    pl.semaphore_wait(barrier, 3 + (z + Z - 1) // Z + (2 * Z - 2 - z) // Z)


def gather_kernel(width, x_ref, rows_ref, *refs):
    o_ref, pile, send_sem, recv_sem = refs[-4:]
    y, z, x, c = place()
    halves = (pl.ds(0, CUT), pl.ds(CUT, width - CUT))
    half = rows_ref.shape[1] // 2
    step = half // 4
    o_ref[y * 8 + z * 2 + x, c] = x_ref[...]
    greet()

    def copy(q, core, h, way, target, stream):
        tile = o_ref.at[q, core, :, halves[h]]
        return pltpu.make_async_remote_copy(
            src_ref=tile,
            dst_ref=tile,
            send_sem=send_sem.at[q, h, way],
            recv_sem=recv_sem.at[q, h, stream],
            device_id=target,
            device_id_type=MESH,
        )

    other = device(y, z, x, 1 - c)

    def unpack(q):
        one = o_ref[q, 0, :, :half].astype(jnp.float32)
        two = o_ref[q, 1, :, :half].astype(jnp.float32)
        to = pl.ds(pl.multiple_of(q * 16, 16), 16)
        rows_ref[to, :half] = jnp.concatenate([one[:8], two[:8]], axis=0).astype(jnp.bfloat16)
        rows_ref[to, half:] = jnp.concatenate([one[8:], two[8:]], axis=0).astype(jnp.bfloat16)

    def visit(flips, drain, k):
        dz = offset_of(k)
        zs = z + dz

        def run(q, h, way, target):
            made = copy(q, c, h, way, target, 1 if way == 0 else 0)
            if drain:
                made.wait_send()
            else:
                made.start()

        @pl.when((zs >= 0) & (zs < Z))
        def _():
            for fx, fy in flips:
                q = (1 - y if fy else y) * 8 + zs * 2 + (1 - x if fx else x)
                for h in (0, 1):
                    if not drain:
                        landed = copy(q, c, h, 0, other, 0)
                        if fx or fy:
                            landed.wait_recv()
                        else:
                            pl.when(dz != 0)(landed.wait_recv)
                    if not fx and not fy:
                        pl.when((dz >= 0) & (z >= 1))(lambda: run(q, h, 4, device(y, z - 1, x, c)))
                        pl.when((dz <= 0) & (z + 1 < Z))(lambda: run(q, h, 3, device(y, z + 1, x, c)))
                    if not fy and (h == 0 or not fx):
                        run(q, h, 1, device(1 - y, z, x, c))
                    if not fx and (h == 1 or not fy):
                        run(q, h, 2, device(y, z, 1 - x, c))
                    run(q, h, 0, other)
                    if drain:
                        copy(q, 1 - c, h, 0, other, 1).wait_recv()
                if drain:
                    unpack(q)

    for drain in (False, True):
        for flips in LEVELS:
            pl.loop(0, 2 * Z - 1)(functools.partial(visit, flips, drain))

    @pl.loop(0, CHIPS // 4)
    def _(g):
        some = o_ref[pl.ds(g * 4, 4), :, :, half : half + step].astype(jnp.float32)
        some = some.reshape(128, step)
        to = pl.ds(pl.multiple_of(CHIPS * 16 + g * 16, 16), 16)
        for i in range(step // 128):
            pile[i] = some[:, i * 128 : (i + 1) * 128]
            for j in range(8):
                part = pile[i, pl.ds(j, 16, stride=8), :].astype(jnp.bfloat16)
                rows_ref[to, j * step + i * 128 : j * step + (i + 1) * 128] = part

    if len(refs) == 5:
        refs[0][...] = o_ref[:, :, :, half + step :]


def gather(block, width, cid):
    count = lax.axis_size("row") * lax.axis_size("vocab")
    packed = width * 5 // 8
    if (lax.axis_size("row"), lax.axis_size("vocab")) != (2, 16):
        every = lax.all_gather(block, ("row", "vocab"), axis=0, tiled=False)
        return spread(every, width), every[:, :, packed:]
    extra = block.shape[1] - packed
    shapes = [jax.ShapeDtypeStruct((count * 10, width), block.dtype)]
    if extra:
        shapes.append(jax.ShapeDtypeStruct((CHIPS, 2, 16, extra), block.dtype))
    out = pl.pallas_call(
        functools.partial(gather_kernel, block.shape[1]),
        out_shape=shapes,
        in_specs=[pl.BlockSpec(memory_space=VMEM)],
        out_specs=[pl.BlockSpec(memory_space=VMEM) for _ in shapes],
        scratch_shapes=[
            VMEM((CHIPS, 2, 16, block.shape[1]), block.dtype),
            VMEM((width // 1024, 128, 128), jnp.float32),
            pltpu.SemaphoreType.DMA((CHIPS, 2, 5)),
            pltpu.SemaphoreType.DMA((CHIPS, 2, 2)),
        ],
        compiler_params=pltpu.CompilerParams(
            collective_id=cid, has_side_effects=True, vmem_limit_bytes=40 * 2**20
        ),
    )(block)
    return out[0], out[1].reshape(count, 16, extra) if extra else None


def scatter_kernel(width, rows_ref, o_ref, p_ref, pile, buf, stage, acc, send_sem, recv_sem):
    y, z, x, c = place()
    halves = (pl.ds(0, CUT), pl.ds(CUT, width - CUT))
    sizes = (CUT, width - CUT)
    other = device(y, z, x, 1 - c)
    half = rows_ref.shape[1] // 2
    step = half // 4

    @pl.loop(0, CHIPS // 4)
    def _(g):
        of = pl.ds(pl.multiple_of(CHIPS * 16 + g * 16, 16), 16)
        for i in range(step // 128):
            for j in range(8):
                part = rows_ref[of, j * step + i * 128 : j * step + (i + 1) * 128]
                pile[i, pl.ds(j, 16, stride=8), :] = part.astype(jnp.float32)
            some = pile[i].reshape(4, 2, 16, 128).astype(jnp.bfloat16)
            p_ref[pl.ds(g * 4, 4), :, :, half + i * 128 : half + (i + 1) * 128] = some

    greet()

    def pack_chip(q):
        of = pl.ds(pl.multiple_of(q * 16, 16), 16)
        left = rows_ref[of, :half].astype(jnp.float32)
        right = rows_ref[of, half:].astype(jnp.float32)
        for core in (0, 1):
            those = slice(core * 8, core * 8 + 8)
            both = jnp.concatenate([left[those], right[those]], axis=0)
            p_ref[q, core, :, :half] = both.astype(jnp.bfloat16)

    def chip(zs, fx, fy):
        return (1 - y if fy else y) * 8 + zs * 2 + (1 - x if fx else x)

    def to_core(q, h):
        return pltpu.make_async_remote_copy(
            src_ref=p_ref.at[q, 1 - c, :, halves[h]],
            dst_ref=buf.at[0, q, :, halves[h]],
            send_sem=send_sem.at[q, h, 0],
            recv_sem=recv_sem.at[q, h, 0],
            device_id=other,
            device_id_type=MESH,
        )

    def to_parent(q, h, way, target):
        return pltpu.make_async_remote_copy(
            src_ref=stage.at[q, :, halves[h]],
            dst_ref=buf.at[way, q, :, halves[h]],
            send_sem=send_sem.at[q, h, 1],
            recv_sem=recv_sem.at[q, h, way],
            device_id=target,
            device_id_type=MESH,
        )

    def visit(flips, phase, i):
        dz = offset_of(2 * Z - 2 - i)
        zs = z + dz

        @pl.when((zs >= 0) & (zs < Z))
        def _():
            for fx, fy in flips:
                q = chip(zs, fx, fy)
                if phase == 0:
                    pack_chip(q)
                for h in (0, 1):
                    if phase == 0:
                        to_core(q, h).start()
                        continue
                    if phase == 1:
                        cols = pl.ds(0, sizes[h])

                        def add(way):
                            to_parent(q, h, way, other).wait_recv()
                            acc[:, cols] += buf[way, q, :, halves[h]].astype(jnp.float32)

                        to_core(q, h).wait_recv()
                        acc[:, cols] = p_ref[q, c, :, halves[h]].astype(jnp.float32) + buf[
                            0, q, :, halves[h]
                        ].astype(jnp.float32)
                        if not fy and (h == 0 or not fx):
                            add(1)
                        if not fx and (h == 1 or not fy):
                            add(2)
                        if not fx and not fy:
                            pl.when((dz >= 0) & (z >= 1))(lambda: add(4))
                            pl.when((dz <= 0) & (z + 1 < Z))(lambda: add(3))

                            @pl.when(dz == 0)
                            def _():
                                o_ref[:, halves[h]] = acc[:, cols]

                        stage[q, :, halves[h]] = acc[:, cols].astype(jnp.bfloat16)
                    else:
                        to_core(q, h).wait_send()

                    def run(way, target):
                        made = to_parent(q, h, way, target)
                        if phase == 1:
                            made.start()
                        else:
                            made.wait_send()

                    if fy and (h == 0 or not fx):
                        run(1, device(1 - y, z, x, c))
                    elif fx:
                        run(2, device(y, z, 1 - x, c))
                    else:
                        pl.when(dz > 0)(lambda: run(4, device(y, z + 1, x, c)))
                        pl.when(dz < 0)(lambda: run(3, device(y, z - 1, x, c)))

    for phase in (0, 1, 2):
        for flips in LEVELS[::-1]:
            pl.loop(0, 2 * Z - 1)(functools.partial(visit, flips, phase))


def scatter(rows, cid):
    count = lax.axis_size("row") * lax.axis_size("vocab")
    if (lax.axis_size("row"), lax.axis_size("vocab")) != (2, 16):
        parts = unspread(rows, count).astype(jnp.float32)
        return lax.psum_scatter(parts, ("row", "vocab"), scatter_dimension=0, tiled=False)
    packed = rows.shape[1] * 5 // 8
    return pl.pallas_call(
        functools.partial(scatter_kernel, packed),
        out_shape=jax.ShapeDtypeStruct((16, packed), jnp.float32),
        in_specs=[pl.BlockSpec(memory_space=VMEM)],
        out_specs=pl.BlockSpec(memory_space=VMEM),
        scratch_shapes=[
            VMEM((CHIPS, 2, 16, packed), jnp.bfloat16),
            VMEM((rows.shape[1] // 1024, 128, 128), jnp.float32),
            VMEM((5, CHIPS, 16, packed), jnp.bfloat16),
            VMEM((CHIPS, 16, packed), jnp.bfloat16),
            VMEM((16, CUT), jnp.float32),
            pltpu.SemaphoreType.DMA((CHIPS, 2, 2)),
            pltpu.SemaphoreType.DMA((CHIPS, 2, 5)),
        ],
        compiler_params=pltpu.CompilerParams(
            collective_id=cid, has_side_effects=True, vmem_limit_bytes=40 * 2**20
        ),
    )(rows)


def exchange_kernel(n_vocab, count, x_ref, o_ref, send_sem, recv_sem):
    me = lax.axis_index("row") * n_vocab + lax.axis_index("vocab")
    barrier = pltpu.get_barrier_semaphore()

    @pl.loop(1, count)
    def _(k):
        peer = (me + k) % count
        pl.semaphore_signal(
            barrier, inc=1, device_id=(peer // n_vocab, peer % n_vocab), device_id_type=MESH
        )

    o_ref[me] = x_ref[...]
    pl.semaphore_wait(barrier, count - 1)

    def copy(k, slot):
        peer = (me + k) % count
        return pltpu.make_async_remote_copy(
            src_ref=x_ref,
            dst_ref=o_ref.at[slot],
            send_sem=send_sem.at[k],
            recv_sem=recv_sem.at[k],
            device_id=(peer // n_vocab, peer % n_vocab),
            device_id_type=MESH,
        )

    @pl.loop(1, count)
    def _(k):
        copy(k, me).start()

    @pl.loop(1, count)
    def _(k):
        copy(k, (me + count - k) % count).wait_recv()
        copy(k, me).wait_send()


def exchange(values, cid):
    size = values.shape[0]
    if (lax.axis_size("row"), lax.axis_size("vocab")) != (2, 16):
        return lax.all_gather(values, ("row", "vocab"), axis=0, tiled=False)
    n_vocab = lax.axis_size("vocab")
    count = lax.axis_size("row") * n_vocab
    rows = -(-size // 1024) * 8
    block = jnp.pad(values, (0, rows * 128 - size)).reshape(rows, 128)
    out = pl.pallas_call(
        functools.partial(exchange_kernel, n_vocab, count),
        out_shape=jax.ShapeDtypeStruct((count, rows, 128), jnp.float32),
        in_specs=[pl.BlockSpec(memory_space=VMEM)],
        out_specs=pl.BlockSpec(memory_space=VMEM),
        scratch_shapes=[
            pltpu.SemaphoreType.DMA((count,)),
            pltpu.SemaphoreType.DMA((count,)),
        ],
        compiler_params=pltpu.CompilerParams(collective_id=cid, has_side_effects=True),
    )(block)
    return out.reshape(count, rows * 128)[:, :size]


def pack(rows):
    lead, width = rows.shape[:-2], rows.shape[-1]
    first = rows[..., :8, :]
    main = jnp.concatenate([first[..., : width // 2], first[..., width // 2 :]], axis=-2)
    rest = rows[..., 8:, :].reshape(lead + (16, width // 8))
    return jnp.concatenate([main, rest], axis=-1)


def spread(blocks, width):
    count = blocks.shape[0]
    half = width // 2
    main = jnp.concatenate(
        [blocks[:, :8, :half].reshape(-1, half), blocks[:, 8:, :half].reshape(-1, half)], axis=1
    )
    rest = blocks[:, :, half : half + width // 8].reshape(count * 2, width)
    return jnp.concatenate([main, rest], axis=0)


def unspread(rows, count):
    width = rows.shape[1]
    half = width // 2
    first = rows[: count * 8].reshape(count, 8, width)
    main = jnp.concatenate([first[:, :, :half], first[:, :, half:]], axis=1)
    rest = rows[count * 8 :].reshape(count, 16, width // 8)
    return jnp.concatenate([main, rest], axis=2)


def in_order(per_row, count):
    table = per_row.reshape(count, 10)
    return jnp.concatenate([table[:, :8].reshape(-1), table[:, 8:].reshape(-1)])


def body(
    tokens,
    norm_gain,
    router,
    routes,
    w_gate,
    w_up,
    w_down,
    head_gain,
    head,
    draft_logits,
    draft_tokens,
    reject_pos,
):
    n_vocab = lax.axis_size("vocab")
    count = lax.axis_size("row") * n_vocab
    width = tokens.shape[1]
    experts = n_vocab
    resid_in = tokens.astype(jnp.float32)
    normed = rms_norm(resid_in, norm_gain).astype(jnp.bfloat16)
    scores = jax.nn.sigmoid(jnp.dot(normed, router, preferred_element_type=jnp.float32))
    member = routes[:, :, None] == jnp.arange(experts, dtype=jnp.int32)[None, None, :]
    picked = jnp.any(member, axis=1).astype(jnp.float32) * scores
    weights = 2.5 * picked / jnp.sum(picked, axis=1, keepdims=True)
    high = lax.reduce_precision(weights, 8, 7)
    low = weights - high
    both = jnp.concatenate([high, low], axis=1).astype(jnp.bfloat16)
    both = jnp.pad(both, ((0, 6), (0, 128 - 2 * experts)))
    x, table = gather(jnp.concatenate([pack(normed), both], axis=1), width, 0)

    table = table[:, :10, : 2 * experts].astype(jnp.float32)
    table = table[:, :, :experts] + table[:, :, experts:]
    mine = jnp.arange(experts, dtype=jnp.int32) == lax.axis_index("vocab")
    row_weight = jnp.sum(jnp.where(mine[None, None, :], table, 0.0), axis=-1)
    row_weight = in_order(row_weight.reshape(-1), count)

    gate_out = jnp.dot(x, w_gate[0], preferred_element_type=jnp.float32)
    up_out = jnp.dot(x, w_up[0], preferred_element_type=jnp.float32)
    hidden = (jax.nn.silu(gate_out) * up_out).astype(jnp.bfloat16)
    down_out = jnp.dot(hidden, w_down[0], preferred_element_type=jnp.float32)
    parts = (down_out * row_weight[:, None]).astype(jnp.bfloat16)
    summed = scatter(parts, 1)

    half = width // 2
    moe_sum = jnp.concatenate(
        [
            jnp.concatenate([summed[:8, :half], summed[8:, :half]], axis=1),
            summed[:, half:].reshape(2, width),
        ],
        axis=0,
    )
    mixed_rows = resid_in + moe_sum
    final_normed = rms_norm(mixed_rows, head_gain).astype(jnp.bfloat16)
    hn, _ = gather(pack(final_normed), width, 2)
    logits = lax.dot_general(
        hn, head, (((1,), (1,)), ((), ())), preferred_element_type=jnp.float32
    )

    local_vocab = head.shape[0]
    requests = draft_tokens.shape[0]
    slots = DRAFTS + 1
    rows = requests * slots
    drafts = requests * DRAFTS
    draft_vals = draft_logits.astype(jnp.float32)
    offset = lax.axis_index(("row", "vocab")) * local_vocab
    lanes = jnp.arange(local_vocab, dtype=jnp.int32)
    local_ids = draft_tokens - offset
    row_ids = in_order(jnp.pad(local_ids, ((0, 0), (0, 1)), constant_values=-1).reshape(-1), count)
    pick_t = jnp.sum(jnp.where(lanes[None, :] == row_ids[:, None], logits, 0.0), axis=-1)
    pick_d = jnp.sum(
        jnp.where(lanes[None, None, :] == local_ids[:, :, None], draft_vals, 0.0), axis=-1
    )
    top_t = jnp.max(logits, axis=-1)
    top_d = jnp.max(draft_vals, axis=-1)
    sum_t = jnp.sum(jnp.exp(logits - top_t[:, None]), axis=-1)
    sum_d = jnp.sum(jnp.exp(draft_vals - top_d[:, :, None]), axis=-1)
    own = [top_t, sum_t, pick_t, top_d.reshape(-1), sum_d.reshape(-1), pick_d.reshape(-1)]
    every = exchange(jnp.concatenate(own), 3)

    def merge(start, size):
        tops = every[:, start : start + size]
        sums = every[:, start + size : start + 2 * size]
        picks = every[:, start + 2 * size : start + 3 * size]
        top = jnp.max(tops, axis=0)
        return top, jnp.sum(sums * jnp.exp(tops - top[None, :]), axis=0), jnp.sum(picks, axis=0)

    top_target, sum_target, pick_target = merge(0, rows)
    top_draft, sum_draft, pick_draft = [
        part.reshape(requests, DRAFTS) for part in merge(3 * rows, drafts)
    ]
    log_draft = pick_draft - top_draft - jnp.log(sum_draft)

    row_at = jnp.arange(requests, dtype=jnp.int32) * slots + reject_pos
    natural = jnp.arange(rows, dtype=jnp.int32)
    order = in_order(natural, count)
    chosen = (row_at[:, None] == order[None, :]).astype(jnp.float32)
    logits_at = jnp.dot(chosen, logits, precision=lax.Precision.HIGHEST)
    top_at = jnp.sum(chosen * top_target[None, :], axis=1)
    sum_at = jnp.sum(chosen * sum_target[None, :], axis=1)
    log_rows = pick_target - top_target - jnp.log(sum_target)
    log_rows = jnp.concatenate(
        [log_rows[: count * 8].reshape(count, 8), log_rows[count * 8 :].reshape(count, 2)], axis=1
    ).reshape(requests, slots)
    accept = jnp.exp(jnp.minimum(log_rows[:, :DRAFTS] - log_draft, 0.0))

    position = jnp.arange(DRAFTS, dtype=jnp.int32)[None, :] == reject_pos[:, None]
    draft_raw = jnp.sum(jnp.where(position[:, :, None], draft_vals, 0.0), axis=1)
    top_d_at = jnp.sum(jnp.where(position, top_draft, 0.0), axis=1)
    sum_d_at = jnp.sum(jnp.where(position, sum_draft, 0.0), axis=1)
    drafted = (reject_pos < DRAFTS)[:, None]
    draft_at = jnp.where(
        drafted, jnp.exp(draft_raw - top_d_at[:, None]) / jnp.where(drafted, sum_d_at[:, None], 1.0), 0.0
    )
    target_at = jnp.exp(logits_at - top_at[:, None]) / sum_at[:, None]
    gap_rows = jnp.maximum(target_at - draft_at, 0.0)
    gap_total = jnp.sum(exchange(jnp.sum(gap_rows, axis=-1), 4), axis=0)
    residual = jnp.sqrt(V * gap_rows / gap_total[:, None])
    return (residual, accept)


def solution(mesh):
    placed = (
        P(("row", "vocab"), None),
        P(),
        P(),
        P(("row", "vocab"), None),
        P("vocab", None, "row"),
        P("vocab", None, "row"),
        P("vocab", "row", None),
        P(),
        P(("row", "vocab"), None),
        P(None, None, ("row", "vocab")),
        P(),
        P(),
    )
    return jax.shard_map(
        body,
        mesh=mesh,
        in_specs=placed,
        out_specs=(P(None, ("row", "vocab")), P()),
        check_vma=False,
    )
```

```python
import functools

import jax
import jax.numpy as jnp
from jax import lax
from jax.experimental import pallas as pl
from jax.experimental.pallas import tpu as pltpu
from jax.sharding import PartitionSpec as P

V = 65536
DRAFTS = 4
MESH = pl.DeviceIdType.MESH
VMEM = pltpu.VMEM
Z = 4
CHIPS = 16
LEVELS = (((0, 0),), ((0, 1), (1, 0)), ((1, 1),))
CUT = 2304


def rms_norm(values, gain):
    return values * lax.rsqrt(jnp.mean(values * values, axis=-1, keepdims=True) + 1e-06) * gain


def place():
    y = lax.axis_index("row")
    v = lax.axis_index("vocab")
    return y, v // 4, (v // 2) % 2, v % 2


def device(y, z, x, c):
    return (y, (z * 2 + x) * 2 + c)


def offset_of(k):
    return ((k + 1) // 2) * (1 - 2 * ((k + 1) % 2))


def greet():
    y, z, x, c = place()
    barrier = pltpu.get_barrier_semaphore()

    def signal(target):
        pl.semaphore_signal(barrier, inc=1, device_id=target, device_id_type=MESH)

    signal(device(y, z, x, 1 - c))
    signal(device(1 - y, z, x, c))
    signal(device(y, z, 1 - x, c))
    pl.when(z + 1 < Z)(lambda: signal(device(y, z + 1, x, c)))
    pl.when(z >= 1)(lambda: signal(device(y, z - 1, x, c)))
    pl.semaphore_wait(barrier, 3 + (z + Z - 1) // Z + (2 * Z - 2 - z) // Z)


def gather_kernel(width, x_ref, rows_ref, *refs):
    o_ref, pile, send_sem, recv_sem = refs[-4:]
    y, z, x, c = place()
    halves = (pl.ds(0, CUT), pl.ds(CUT, width - CUT))
    half = rows_ref.shape[1] // 2
    step = half // 4
    o_ref[y * 8 + z * 2 + x, c] = x_ref[...]
    greet()

    def copy(q, core, h, way, target, stream):
        tile = o_ref.at[q, core, :, halves[h]]
        return pltpu.make_async_remote_copy(
            src_ref=tile,
            dst_ref=tile,
            send_sem=send_sem.at[q, h, way],
            recv_sem=recv_sem.at[q, h, stream],
            device_id=target,
            device_id_type=MESH,
        )

    other = device(y, z, x, 1 - c)

    def unpack(q):
        one = o_ref[q, 0, :, :half].astype(jnp.float32)
        two = o_ref[q, 1, :, :half].astype(jnp.float32)
        to = pl.ds(pl.multiple_of(q * 16, 16), 16)
        rows_ref[to, :half] = jnp.concatenate([one[:8], two[:8]], axis=0).astype(jnp.bfloat16)
        rows_ref[to, half:] = jnp.concatenate([one[8:], two[8:]], axis=0).astype(jnp.bfloat16)

    def visit(flips, drain, k):
        dz = offset_of(k)
        zs = z + dz

        def run(q, h, way, target):
            made = copy(q, c, h, way, target, 1 if way == 0 else 0)
            if drain:
                made.wait_send()
            else:
                made.start()

        @pl.when((zs >= 0) & (zs < Z))
        def _():
            for fx, fy in flips:
                q = (1 - y if fy else y) * 8 + zs * 2 + (1 - x if fx else x)
                for h in (0, 1):
                    if not drain:
                        landed = copy(q, c, h, 0, other, 0)
                        if fx or fy:
                            landed.wait_recv()
                        else:
                            pl.when(dz != 0)(landed.wait_recv)
                    if not fx and not fy:
                        pl.when((dz >= 0) & (z >= 1))(lambda: run(q, h, 4, device(y, z - 1, x, c)))
                        pl.when((dz <= 0) & (z + 1 < Z))(lambda: run(q, h, 3, device(y, z + 1, x, c)))
                    if not fy and (h == 0 or not fx):
                        run(q, h, 1, device(1 - y, z, x, c))
                    if not fx and (h == 1 or not fy):
                        run(q, h, 2, device(y, z, 1 - x, c))
                    run(q, h, 0, other)
                    if drain:
                        copy(q, 1 - c, h, 0, other, 1).wait_recv()
                if drain:
                    unpack(q)

    for drain in (False, True):
        for flips in LEVELS:
            pl.loop(0, 2 * Z - 1)(functools.partial(visit, flips, drain))

    @pl.loop(0, CHIPS // 4)
    def _(g):
        some = o_ref[pl.ds(g * 4, 4), :, :, half : half + step].astype(jnp.float32)
        some = some.reshape(128, step)
        to = pl.ds(pl.multiple_of(CHIPS * 16 + g * 16, 16), 16)
        for i in range(step // 128):
            pile[i] = some[:, i * 128 : (i + 1) * 128]
            for j in range(8):
                part = pile[i, pl.ds(j, 16, stride=8), :].astype(jnp.bfloat16)
                rows_ref[to, j * step + i * 128 : j * step + (i + 1) * 128] = part

    if len(refs) == 5:
        refs[0][...] = o_ref[:, :, :, half + step :]


def gather(block, width, cid):
    count = lax.axis_size("row") * lax.axis_size("vocab")
    packed = width * 5 // 8
    if (lax.axis_size("row"), lax.axis_size("vocab")) != (2, 16):
        every = lax.all_gather(block, ("row", "vocab"), axis=0, tiled=False)
        return spread(every, width), every[:, :, packed:]
    extra = block.shape[1] - packed
    shapes = [jax.ShapeDtypeStruct((count * 10, width), block.dtype)]
    if extra:
        shapes.append(jax.ShapeDtypeStruct((CHIPS, 2, 16, extra), block.dtype))
    out = pl.pallas_call(
        functools.partial(gather_kernel, block.shape[1]),
        out_shape=shapes,
        in_specs=[pl.BlockSpec(memory_space=VMEM)],
        out_specs=[pl.BlockSpec(memory_space=VMEM) for _ in shapes],
        scratch_shapes=[
            VMEM((CHIPS, 2, 16, block.shape[1]), block.dtype),
            VMEM((width // 1024, 128, 128), jnp.float32),
            pltpu.SemaphoreType.DMA((CHIPS, 2, 5)),
            pltpu.SemaphoreType.DMA((CHIPS, 2, 2)),
        ],
        compiler_params=pltpu.CompilerParams(
            collective_id=cid, has_side_effects=True, vmem_limit_bytes=40 * 2**20
        ),
    )(block)
    return out[0], out[1].reshape(count, 16, extra) if extra else None


def scatter_kernel(width, rows_ref, o_ref, p_ref, pile, buf, stage, acc, send_sem, recv_sem):
    y, z, x, c = place()
    halves = (pl.ds(0, CUT), pl.ds(CUT, width - CUT))
    sizes = (CUT, width - CUT)
    other = device(y, z, x, 1 - c)
    half = rows_ref.shape[1] // 2
    step = half // 4

    @pl.loop(0, CHIPS // 4)
    def _(g):
        of = pl.ds(pl.multiple_of(CHIPS * 16 + g * 16, 16), 16)
        for i in range(step // 128):
            for j in range(8):
                part = rows_ref[of, j * step + i * 128 : j * step + (i + 1) * 128]
                pile[i, pl.ds(j, 16, stride=8), :] = part.astype(jnp.float32)
            some = pile[i].reshape(4, 2, 16, 128).astype(jnp.bfloat16)
            p_ref[pl.ds(g * 4, 4), :, :, half + i * 128 : half + (i + 1) * 128] = some

    greet()

    def pack_chip(q):
        of = pl.ds(pl.multiple_of(q * 16, 16), 16)
        left = rows_ref[of, :half].astype(jnp.float32)
        right = rows_ref[of, half:].astype(jnp.float32)
        for core in (0, 1):
            those = slice(core * 8, core * 8 + 8)
            both = jnp.concatenate([left[those], right[those]], axis=0)
            p_ref[q, core, :, :half] = both.astype(jnp.bfloat16)

    def chip(zs, fx, fy):
        return (1 - y if fy else y) * 8 + zs * 2 + (1 - x if fx else x)

    def to_core(q, h):
        return pltpu.make_async_remote_copy(
            src_ref=p_ref.at[q, 1 - c, :, halves[h]],
            dst_ref=buf.at[0, q, :, halves[h]],
            send_sem=send_sem.at[q, h, 0],
            recv_sem=recv_sem.at[q, h, 0],
            device_id=other,
            device_id_type=MESH,
        )

    def to_parent(q, h, way, target):
        return pltpu.make_async_remote_copy(
            src_ref=stage.at[q, :, halves[h]],
            dst_ref=buf.at[way, q, :, halves[h]],
            send_sem=send_sem.at[q, h, 1],
            recv_sem=recv_sem.at[q, h, way],
            device_id=target,
            device_id_type=MESH,
        )

    def visit(flips, phase, i):
        dz = offset_of(2 * Z - 2 - i)
        zs = z + dz

        @pl.when((zs >= 0) & (zs < Z))
        def _():
            for fx, fy in flips:
                q = chip(zs, fx, fy)
                if phase == 0:
                    pack_chip(q)
                for h in (0, 1):
                    if phase == 0:
                        to_core(q, h).start()
                        continue
                    if phase == 1:
                        cols = pl.ds(0, sizes[h])

                        def add(way):
                            to_parent(q, h, way, other).wait_recv()
                            acc[:, cols] += buf[way, q, :, halves[h]].astype(jnp.float32)

                        to_core(q, h).wait_recv()
                        acc[:, cols] = p_ref[q, c, :, halves[h]].astype(jnp.float32) + buf[
                            0, q, :, halves[h]
                        ].astype(jnp.float32)
                        if not fy and (h == 0 or not fx):
                            add(1)
                        if not fx and (h == 1 or not fy):
                            add(2)
                        if not fx and not fy:
                            pl.when((dz >= 0) & (z >= 1))(lambda: add(4))
                            pl.when((dz <= 0) & (z + 1 < Z))(lambda: add(3))

                            @pl.when(dz == 0)
                            def _():
                                o_ref[:, halves[h]] = acc[:, cols]

                        stage[q, :, halves[h]] = acc[:, cols].astype(jnp.bfloat16)
                    else:
                        to_core(q, h).wait_send()

                    def run(way, target):
                        made = to_parent(q, h, way, target)
                        if phase == 1:
                            made.start()
                        else:
                            made.wait_send()

                    if fy and (h == 0 or not fx):
                        run(1, device(1 - y, z, x, c))
                    elif fx:
                        run(2, device(y, z, 1 - x, c))
                    else:
                        pl.when(dz > 0)(lambda: run(4, device(y, z + 1, x, c)))
                        pl.when(dz < 0)(lambda: run(3, device(y, z - 1, x, c)))

    for phase in (0, 1, 2):
        for flips in LEVELS[::-1]:
            pl.loop(0, 2 * Z - 1)(functools.partial(visit, flips, phase))


def scatter(rows, cid):
    count = lax.axis_size("row") * lax.axis_size("vocab")
    if (lax.axis_size("row"), lax.axis_size("vocab")) != (2, 16):
        parts = unspread(rows, count).astype(jnp.float32)
        return lax.psum_scatter(parts, ("row", "vocab"), scatter_dimension=0, tiled=False)
    packed = rows.shape[1] * 5 // 8
    return pl.pallas_call(
        functools.partial(scatter_kernel, packed),
        out_shape=jax.ShapeDtypeStruct((16, packed), jnp.float32),
        in_specs=[pl.BlockSpec(memory_space=VMEM)],
        out_specs=pl.BlockSpec(memory_space=VMEM),
        scratch_shapes=[
            VMEM((CHIPS, 2, 16, packed), jnp.bfloat16),
            VMEM((rows.shape[1] // 1024, 128, 128), jnp.float32),
            VMEM((5, CHIPS, 16, packed), jnp.bfloat16),
            VMEM((CHIPS, 16, packed), jnp.bfloat16),
            VMEM((16, CUT), jnp.float32),
            pltpu.SemaphoreType.DMA((CHIPS, 2, 2)),
            pltpu.SemaphoreType.DMA((CHIPS, 2, 5)),
        ],
        compiler_params=pltpu.CompilerParams(
            collective_id=cid, has_side_effects=True, vmem_limit_bytes=40 * 2**20
        ),
    )(rows)


def exchange_kernel(n_vocab, count, x_ref, o_ref, send_sem, recv_sem):
    me = lax.axis_index("row") * n_vocab + lax.axis_index("vocab")
    barrier = pltpu.get_barrier_semaphore()

    @pl.loop(1, count)
    def _(k):
        peer = (me + k) % count
        pl.semaphore_signal(
            barrier, inc=1, device_id=(peer // n_vocab, peer % n_vocab), device_id_type=MESH
        )

    o_ref[me] = x_ref[...]
    pl.semaphore_wait(barrier, count - 1)

    def copy(k, slot):
        peer = (me + k) % count
        return pltpu.make_async_remote_copy(
            src_ref=x_ref,
            dst_ref=o_ref.at[slot],
            send_sem=send_sem.at[k],
            recv_sem=recv_sem.at[k],
            device_id=(peer // n_vocab, peer % n_vocab),
            device_id_type=MESH,
        )

    @pl.loop(1, count)
    def _(k):
        copy(k, me).start()

    @pl.loop(1, count)
    def _(k):
        copy(k, (me + count - k) % count).wait_recv()
        copy(k, me).wait_send()


def exchange(values, cid):
    size = values.shape[0]
    if (lax.axis_size("row"), lax.axis_size("vocab")) != (2, 16):
        return lax.all_gather(values, ("row", "vocab"), axis=0, tiled=False)
    n_vocab = lax.axis_size("vocab")
    count = lax.axis_size("row") * n_vocab
    rows = -(-size // 1024) * 8
    block = jnp.pad(values, (0, rows * 128 - size)).reshape(rows, 128)
    out = pl.pallas_call(
        functools.partial(exchange_kernel, n_vocab, count),
        out_shape=jax.ShapeDtypeStruct((count, rows, 128), jnp.float32),
        in_specs=[pl.BlockSpec(memory_space=VMEM)],
        out_specs=pl.BlockSpec(memory_space=VMEM),
        scratch_shapes=[
            pltpu.SemaphoreType.DMA((count,)),
            pltpu.SemaphoreType.DMA((count,)),
        ],
        compiler_params=pltpu.CompilerParams(collective_id=cid, has_side_effects=True),
    )(block)
    return out.reshape(count, rows * 128)[:, :size]


def hidden_kernel(x_ref, gate_ref, up_ref, o_ref, gate_sum, up_sum):
    step = pl.program_id(0)

    @pl.when(step == 0)
    def _():
        gate_sum[...] = jnp.zeros_like(gate_sum)
        up_sum[...] = jnp.zeros_like(up_sum)

    x = x_ref[...]
    gate_sum[...] += jnp.dot(x, gate_ref[...], preferred_element_type=jnp.float32)
    up_sum[...] += jnp.dot(x, up_ref[...], preferred_element_type=jnp.float32)

    @pl.when(step == pl.num_programs(0) - 1)
    def _():
        gate = gate_sum[...]
        o_ref[...] = (gate / (1.0 + jnp.exp(-gate)) * up_sum[...]).astype(jnp.bfloat16)


def hidden_units(x, gate_w, up_w):
    rows, width = x.shape
    units = gate_w.shape[1]
    if (lax.axis_size("row"), lax.axis_size("vocab")) != (2, 16):
        gate_out = jnp.dot(x, gate_w, preferred_element_type=jnp.float32)
        up_out = jnp.dot(x, up_w, preferred_element_type=jnp.float32)
        return (jax.nn.silu(gate_out) * up_out).astype(jnp.bfloat16)
    depth = width // 7
    return pl.pallas_call(
        hidden_kernel,
        out_shape=jax.ShapeDtypeStruct((rows, units), jnp.bfloat16),
        grid=(7,),
        in_specs=[
            pl.BlockSpec((rows, depth), lambda i: (0, i)),
            pl.BlockSpec((depth, units), lambda i: (i, 0)),
            pl.BlockSpec((depth, units), lambda i: (i, 0)),
        ],
        out_specs=pl.BlockSpec((rows, units), lambda i: (0, 0)),
        scratch_shapes=[VMEM((rows, units), jnp.float32), VMEM((rows, units), jnp.float32)],
        compiler_params=pltpu.CompilerParams(vmem_limit_bytes=40 * 2**20),
        cost_estimate=pl.CostEstimate(
            flops=4 * rows * width * units,
            bytes_accessed=2 * width * (2 * units + rows),
            transcendentals=rows * units,
        ),
    )(x, gate_w, up_w)


def head_kernel(x_ref, head_ref, o_ref):
    o_ref[...] = lax.dot_general(
        x_ref[...], head_ref[...], (((1,), (1,)), ((), ())), preferred_element_type=jnp.float32
    )


def head_logits(x, head):
    rows, width = x.shape
    entries = head.shape[0]
    if (lax.axis_size("row"), lax.axis_size("vocab")) != (2, 16):
        return lax.dot_general(
            x, head, (((1,), (1,)), ((), ())), preferred_element_type=jnp.float32
        )
    return pl.pallas_call(
        head_kernel,
        out_shape=jax.ShapeDtypeStruct((rows, entries), jnp.float32),
        grid=(entries // 256,),
        in_specs=[
            pl.BlockSpec((rows, width), lambda i: (0, 0)),
            pl.BlockSpec((256, width), lambda i: (i, 0)),
        ],
        out_specs=pl.BlockSpec((rows, 256), lambda i: (0, i)),
        compiler_params=pltpu.CompilerParams(vmem_limit_bytes=40 * 2**20),
        cost_estimate=pl.CostEstimate(
            flops=2 * rows * width * entries,
            bytes_accessed=2 * width * (entries + rows) + 4 * rows * entries,
            transcendentals=0,
        ),
    )(x, head)


def pack(rows):
    lead, width = rows.shape[:-2], rows.shape[-1]
    first = rows[..., :8, :]
    main = jnp.concatenate([first[..., : width // 2], first[..., width // 2 :]], axis=-2)
    rest = rows[..., 8:, :].reshape(lead + (16, width // 8))
    return jnp.concatenate([main, rest], axis=-1)


def spread(blocks, width):
    count = blocks.shape[0]
    half = width // 2
    main = jnp.concatenate(
        [blocks[:, :8, :half].reshape(-1, half), blocks[:, 8:, :half].reshape(-1, half)], axis=1
    )
    rest = blocks[:, :, half : half + width // 8].reshape(count * 2, width)
    return jnp.concatenate([main, rest], axis=0)


def unspread(rows, count):
    width = rows.shape[1]
    half = width // 2
    first = rows[: count * 8].reshape(count, 8, width)
    main = jnp.concatenate([first[:, :, :half], first[:, :, half:]], axis=1)
    rest = rows[count * 8 :].reshape(count, 16, width // 8)
    return jnp.concatenate([main, rest], axis=2)


def in_order(per_row, count):
    table = per_row.reshape(count, 10)
    return jnp.concatenate([table[:, :8].reshape(-1), table[:, 8:].reshape(-1)])


def body(
    tokens,
    norm_gain,
    router,
    routes,
    w_gate,
    w_up,
    w_down,
    head_gain,
    head,
    draft_logits,
    draft_tokens,
    reject_pos,
):
    n_vocab = lax.axis_size("vocab")
    count = lax.axis_size("row") * n_vocab
    width = tokens.shape[1]
    experts = n_vocab
    resid_in = tokens.astype(jnp.float32)
    normed = rms_norm(resid_in, norm_gain).astype(jnp.bfloat16)
    scores = jax.nn.sigmoid(jnp.dot(normed, router, preferred_element_type=jnp.float32))
    member = routes[:, :, None] == jnp.arange(experts, dtype=jnp.int32)[None, None, :]
    picked = jnp.any(member, axis=1).astype(jnp.float32) * scores
    weights = 2.5 * picked / jnp.sum(picked, axis=1, keepdims=True)
    high = lax.reduce_precision(weights, 8, 7)
    low = weights - high
    both = jnp.concatenate([high, low], axis=1).astype(jnp.bfloat16)
    both = jnp.pad(both, ((0, 6), (0, 128 - 2 * experts)))
    x, table = gather(jnp.concatenate([pack(normed), both], axis=1), width, 0)

    table = table[:, :10, : 2 * experts].astype(jnp.float32)
    table = table[:, :, :experts] + table[:, :, experts:]
    mine = jnp.arange(experts, dtype=jnp.int32) == lax.axis_index("vocab")
    row_weight = jnp.sum(jnp.where(mine[None, None, :], table, 0.0), axis=-1)
    row_weight = in_order(row_weight.reshape(-1), count)

    hidden = hidden_units(x, w_gate[0], w_up[0])
    down_out = jnp.dot(hidden, w_down[0], preferred_element_type=jnp.float32)
    parts = (down_out * row_weight[:, None]).astype(jnp.bfloat16)
    summed = scatter(parts, 1)

    half = width // 2
    moe_sum = jnp.concatenate(
        [
            jnp.concatenate([summed[:8, :half], summed[8:, :half]], axis=1),
            summed[:, half:].reshape(2, width),
        ],
        axis=0,
    )
    mixed_rows = resid_in + moe_sum
    final_normed = rms_norm(mixed_rows, head_gain).astype(jnp.bfloat16)
    hn, _ = gather(pack(final_normed), width, 2)
    logits = head_logits(hn, head)

    local_vocab = head.shape[0]
    requests = draft_tokens.shape[0]
    slots = DRAFTS + 1
    rows = requests * slots
    drafts = requests * DRAFTS
    draft_vals = draft_logits.astype(jnp.float32)
    offset = lax.axis_index(("row", "vocab")) * local_vocab
    lanes = jnp.arange(local_vocab, dtype=jnp.int32)
    local_ids = draft_tokens - offset
    row_ids = in_order(jnp.pad(local_ids, ((0, 0), (0, 1)), constant_values=-1).reshape(-1), count)
    pick_t = jnp.sum(jnp.where(lanes[None, :] == row_ids[:, None], logits, 0.0), axis=-1)
    pick_d = jnp.sum(
        jnp.where(lanes[None, None, :] == local_ids[:, :, None], draft_vals, 0.0), axis=-1
    )
    top_t = jnp.max(logits, axis=-1)
    top_d = jnp.max(draft_vals, axis=-1)
    sum_t = jnp.sum(jnp.exp(logits - top_t[:, None]), axis=-1)
    sum_d = jnp.sum(jnp.exp(draft_vals - top_d[:, :, None]), axis=-1)
    own = [top_t, sum_t, pick_t, top_d.reshape(-1), sum_d.reshape(-1), pick_d.reshape(-1)]
    every = exchange(jnp.concatenate(own), 3)

    def merge(start, size):
        tops = every[:, start : start + size]
        sums = every[:, start + size : start + 2 * size]
        picks = every[:, start + 2 * size : start + 3 * size]
        top = jnp.max(tops, axis=0)
        return top, jnp.sum(sums * jnp.exp(tops - top[None, :]), axis=0), jnp.sum(picks, axis=0)

    top_target, sum_target, pick_target = merge(0, rows)
    top_draft, sum_draft, pick_draft = [
        part.reshape(requests, DRAFTS) for part in merge(3 * rows, drafts)
    ]
    log_draft = pick_draft - top_draft - jnp.log(sum_draft)

    row_at = jnp.arange(requests, dtype=jnp.int32) * slots + reject_pos
    natural = jnp.arange(rows, dtype=jnp.int32)
    order = in_order(natural, count)
    chosen = (row_at[:, None] == order[None, :]).astype(jnp.float32)
    logits_at = jnp.dot(chosen, logits, precision=lax.Precision.HIGHEST)
    top_at = jnp.sum(chosen * top_target[None, :], axis=1)
    sum_at = jnp.sum(chosen * sum_target[None, :], axis=1)
    log_rows = pick_target - top_target - jnp.log(sum_target)
    log_rows = jnp.concatenate(
        [log_rows[: count * 8].reshape(count, 8), log_rows[count * 8 :].reshape(count, 2)], axis=1
    ).reshape(requests, slots)
    accept = jnp.exp(jnp.minimum(log_rows[:, :DRAFTS] - log_draft, 0.0))

    position = jnp.arange(DRAFTS, dtype=jnp.int32)[None, :] == reject_pos[:, None]
    draft_raw = jnp.sum(jnp.where(position[:, :, None], draft_vals, 0.0), axis=1)
    top_d_at = jnp.sum(jnp.where(position, top_draft, 0.0), axis=1)
    sum_d_at = jnp.sum(jnp.where(position, sum_draft, 0.0), axis=1)
    drafted = (reject_pos < DRAFTS)[:, None]
    draft_at = jnp.where(
        drafted, jnp.exp(draft_raw - top_d_at[:, None]) / jnp.where(drafted, sum_d_at[:, None], 1.0), 0.0
    )
    target_at = jnp.exp(logits_at - top_at[:, None]) / sum_at[:, None]
    gap_rows = jnp.maximum(target_at - draft_at, 0.0)
    gap_total = jnp.sum(exchange(jnp.sum(gap_rows, axis=-1), 4), axis=0)
    residual = jnp.sqrt(V * gap_rows / gap_total[:, None])
    return (residual, accept)


def solution(mesh):
    placed = (
        P(("row", "vocab"), None),
        P(),
        P(),
        P(("row", "vocab"), None),
        P("vocab", None, "row"),
        P("vocab", None, "row"),
        P("vocab", "row", None),
        P(),
        P(("row", "vocab"), None),
        P(None, None, ("row", "vocab")),
        P(),
        P(),
    )
    return jax.shard_map(
        body,
        mesh=mesh,
        in_specs=placed,
        out_specs=(P(None, ("row", "vocab")), P()),
        check_vma=False,
    )
```
